32 devices in a mesh: month: 4 (over y, core), cols: 8 (over z, x).
Axes of the slice: x: 2, y: 2, z: 4, core: 2. Of those that a mesh axis runs over, the one named last changes fastest.
Arguments:
- forcing: float32 [4, 128, 6, 128], P('month', 'cols'), may hold values from -6 to 6
- tiles: bfloat16 [4, 2048, 128, 128], P('month', 'cols'), may hold values from -0.21875 to 0.21875
- tile_rows: int32 [4, 2048], P('month', 'cols'), may hold values from 0 to 127, as said below
- tile_cols: int32 [4, 2048], P('month', 'cols'), may hold values from 0 to 127, as said below
- tile_count: int32 [4, 8], P('month', 'cols'), may hold values from 1 to 256, as said below
- depth: int32 [128, 16], P('cols'), may hold values from 1 to 8
Outputs:
- adjoint: float32 [4, 128, 6, 128], P('month', 'cols')
The draws below stay inside these ranges and needn't reach their ends.
Inputs may be any that keep to these rules, and one draw needn't show every extreme that they name: `tile_cols`: the tiles held by cols index c take their column blocks from c's own blocks, c * 16 to (c + 1) * 16 - 1. `tile_rows`: the tiles held by cols index c take their row blocks from the blocks of c, of its two neighbours c - 1 and c + 1, and of the index c + 4, all counted modulo 128 / 16. `tile_count`: in each month one cols index has all 256 slots live; slots from the count on are unused.
All inputs are finite; a program needn't handle non-finite values.
Results may differ from the reference program's by a relative error of at most 0.022.
Values may be sent and summed in bfloat16 or wider, within the bound.
No kernel may reach another device: no remote copies, remote signals or barrier semaphores. Data moves between devices by JAX's collectives and lax.ppermute only.
A program may use at most 64 MiB of HBM per device.

```python
import jax
import jax.numpy as jnp

BLOCK = 128
LEVELS = 8
TRACERS = 6
BLK_DEV = 16
TILE_DEV = 256
MONTHS = 4
NBLK = 128


def draw_tile_rows(key, part):
    slots = NBLK * TILE_DEV // BLK_DEV
    owners = NBLK // BLK_DEV
    slot = jnp.arange(slots, dtype=jnp.int32)
    owner = slot // TILE_DEV
    side = jax.random.randint(jax.random.fold_in(key, 11), (MONTHS, slots), 0, 4, dtype=jnp.int32)
    side = jnp.where((slot % TILE_DEV == 0)[None, :], 3, side)
    delta = jnp.where(side == 1, -1, jnp.where(side == 2, 1, jnp.where(side == 3, owners // 2, 0))).astype(jnp.int32)
    target = (owner[None, :] + delta + owners) % owners
    offset = jax.random.randint(jax.random.fold_in(key, 13), (MONTHS, slots), 0, BLK_DEV, dtype=jnp.int32)
    return (target * BLK_DEV + offset).astype(jnp.int32)


def draw_tile_cols(key, part):
    slots = NBLK * TILE_DEV // BLK_DEV
    owner = jnp.arange(slots, dtype=jnp.int32) // TILE_DEV
    offset = jax.random.randint(jax.random.fold_in(key, 17), (MONTHS, slots), 0, BLK_DEV, dtype=jnp.int32)
    return (owner[None, :] * BLK_DEV + offset).astype(jnp.int32)


def draw_tile_count(key, part):
    owners = NBLK // BLK_DEV
    base = jax.random.randint(jax.random.fold_in(key, 3), (MONTHS, owners), 1, TILE_DEV // 2 + 1, dtype=jnp.int32)
    pick = jax.random.randint(jax.random.fold_in(key, 5), (MONTHS, 1), 0, owners, dtype=jnp.int32)
    where_top = jnp.arange(owners, dtype=jnp.int32)[None, :] == pick
    return jnp.where(where_top, TILE_DEV, base).astype(jnp.int32)


def place_ends(result, own_key, low, high):
    longest = result.shape.index(max(result.shape))
    spots = []
    for shift in (0, 1):
        where = [jax.random.randint(jax.random.fold_in(own_key, axis), (), 0, length) for axis, length in enumerate(result.shape)]
        where[longest] = (where[longest] + shift) % result.shape[longest]
        spots.append(tuple(where))
    return result.at[spots[0]].set(low).at[spots[1]].set(high)


def block_scale(rng, extent, cuts, least, largest):
    level = 1.0
    for position, blocks in cuts:
        draws = jax.random.uniform(jax.random.fold_in(jax.random.fold_in(rng, 6), position), (blocks,), jnp.float32, least / len(cuts), largest / len(cuts))
        level = level * jnp.repeat(jnp.exp(draws), extent[position] // blocks).reshape((-1,) + (1,) * (len(extent) - 1 - position))
    return level


def scatter_about(own_key, extent, deviation, most, shards=(), held_as=jnp.bfloat16):
    loudness = block_scale(own_key, extent, shards, -0.22, 0.18) if shards else 1.0
    entries = jax.random.normal(own_key, extent, jnp.float32) * deviation * loudness
    return jnp.minimum(jnp.maximum(entries, -most), most).astype(held_as)


def setup_inputs(seed: int = 0) -> dict:
    splits = jax.random.split(jax.random.key(seed), 7)
    return {
        "forcing": scatter_about(splits[0], (MONTHS, NBLK, TRACERS, BLOCK), 1.0, 6.0, ((0, 4), (1, 8)), jnp.float32),
        "tiles": scatter_about(splits[1], (MONTHS, NBLK * TILE_DEV // BLK_DEV, BLOCK, BLOCK), (BLOCK * TILE_DEV // (3 * BLK_DEV)) ** -0.5, 0.21875, ((0, 4), (1, 8))),
        "tile_rows": draw_tile_rows(jax.random.fold_in(splits[6], 71), 0),
        "tile_cols": draw_tile_cols(jax.random.fold_in(splits[6], 71), 0),
        "tile_count": draw_tile_count(jax.random.fold_in(splits[6], 71), 0),
        "depth": place_ends(jax.random.randint(splits[5], (NBLK, BLOCK // LEVELS), 1, LEVELS + 1), jax.random.fold_in(splits[5], 1), 1, LEVELS).astype(jnp.int32),
    }


def wet_mask(depth):
    width = depth.shape[1]
    level = jnp.arange(BLOCK, dtype=jnp.int32) // width
    spread = jnp.tile(depth, (1, LEVELS))
    return (level[None, :] < spread).astype(jnp.float32)[:, None, :]


def month_step(state, forcing_m, tiles_m, rows_m, cols_m, count_m, wet):
    x_vals = (state + forcing_m).astype(jnp.bfloat16)
    picked = x_vals[cols_m].astype(jnp.float32)
    terms = jnp.einsum("stj,sij->sti", picked, tiles_m.astype(jnp.float32))
    slot = jnp.arange(rows_m.shape[0], dtype=jnp.int32)
    live = ((slot % TILE_DEV) < count_m[slot // TILE_DEV]).astype(jnp.float32)
    terms = terms * live[:, None, None]
    summed = jnp.zeros(state.shape, jnp.float32).at[rows_m].add(terms)
    return wet * summed


def reference(forcing, tiles, tile_rows, tile_cols, tile_count, depth):
    wet = wet_mask(depth)
    state = jnp.zeros(forcing.shape[1:], jnp.float32)
    results = [None] * MONTHS
    for sweep in range(2):
        for month in range(MONTHS - 1, -1, -1):
            state = month_step(state, forcing[month], tiles[month], tile_rows[month], tile_cols[month], tile_count[month], wet)
            if sweep == 1:
                results[month] = state
    return jnp.stack(results)
```

```python
import functools

import jax
import jax.numpy as jnp
from jax import lax
from jax.experimental import pallas as pl
from jax.experimental.pallas import tpu as pltpu
from jax.sharding import PartitionSpec as P

SUB = 8
GROUP = 64
NT = (((1,), (1,)), ((), ()))


def wet_mask(depth, block):
    width = depth.shape[1]
    level = jnp.arange(block, dtype=jnp.int32) // width
    spread = jnp.tile(depth, (1, block // width))
    return (level[None, :] < spread).astype(jnp.float32)


def padded(values, rows):
    blocks, tracers, block = values.shape
    values = jnp.pad(values, ((0, 0), (0, rows - tracers), (0, 0)))
    return values.reshape(blocks * rows, block)


def products(live, slots, tiles, x, acc):
    acc[...] = jnp.zeros_like(acc)
    block = tiles.shape[-1]

    def round_of(g, carry):
        first = g * GROUP
        terms = []
        for u in range(0, GROUP, 2):
            s = first + u
            pair = jnp.concatenate([x[slots[1, s]], x[slots[1, s + 1]]], axis=0)
            both = tiles[pl.ds(s, 2)].reshape(2 * block, block)
            terms.append(
                lax.dot_general(pair.astype(jnp.bfloat16), both, NT, preferred_element_type=jnp.float32)
            )
        for u in range(0, GROUP, 2):
            s = first + u
            term = terms[u // 2]
            acc[slots[0, s]] += term[:SUB, :block]
            acc[slots[0, s + 1]] += term[SUB:, block:]
        return carry

    lax.fori_loop(0, (live + GROUP - 1) // GROUP, round_of, 0)


def step_kernel(first, live, slots, wet, forcing, tiles, *refs):
    refs = list(refs)
    arrived = [] if first else [refs.pop(0) for _ in range(4)]
    x, acc = refs[-2:]
    outs = refs[:4]
    own = x.shape[0]

    @pl.when(live[0] > 0)
    def _():
        if first:
            total = forcing[...]
        else:
            state = arrived[0][...].astype(jnp.float32)
            for ref in arrived[1:]:
                state += ref[...].astype(jnp.float32)
            state *= wet[...]
            refs[4][...] = state
            total = state + forcing[...]
        x[...] = total.reshape(x.shape)
        products(live[0], slots, tiles, x, acc)
        for d, out in enumerate(outs):
            out[...] = acc[pl.ds(d * own, own)].reshape(out.shape).astype(out.dtype)


def month_terms(live, slots, wet, forcing, tiles, arrived):
    rows, block = forcing.shape
    own = rows // SUB
    in_vmem = pl.BlockSpec(memory_space=pltpu.VMEM)
    in_smem = pl.BlockSpec(memory_space=pltpu.SMEM)
    first = arrived is None
    out_shape = [jax.ShapeDtypeStruct((rows, block), jnp.bfloat16)] * 4
    if not first:
        out_shape = out_shape + [jax.ShapeDtypeStruct((rows, block), jnp.float32)]
    operands = [live, slots, wet, forcing, tiles] + ([] if first else list(arrived))
    result = pl.pallas_call(
        functools.partial(step_kernel, first),
        out_shape=out_shape,
        in_specs=[in_smem] * 2 + [in_vmem] * (len(operands) - 2),
        out_specs=[in_vmem] * len(out_shape),
        scratch_shapes=[
            pltpu.VMEM((own, SUB, block), jnp.float32),
            pltpu.VMEM((4 * own + 1, SUB, block), jnp.float32),
        ],
        compiler_params=pltpu.CompilerParams(vmem_limit_bytes=16 * 2**20),
    )(*operands)
    return result[:4], (None if first else result[4])


def idle_chain(active, months):
    to = (active - 1) % months
    if months != 4:
        return [(to - k) % months for k in range(1, months - 1)]
    if active ^ 1 == to:
        return [to ^ 2, to ^ 3]
    return [to ^ 1, active ^ 1]


def hops(active, months, ncols, move):
    chain = [(active - 1) % months] + idle_chain(active, months) + [active]
    pairs = [(active * ncols + c, chain[0] * ncols + move(c) % ncols) for c in range(ncols)]
    for source, target in zip(chain, chain[1:]):
        pairs += [(source * ncols + c, target * ncols + c) for c in range(ncols)]
    return pairs


def on_device(forcing, tiles, tile_rows, tile_cols, tile_count, depth):
    months = lax.axis_size("month")
    my_month = lax.axis_index("month")
    ncols = lax.axis_size("cols")
    my_cols = lax.axis_index("cols")
    own, tracers, block = forcing.shape[1:]
    axes = ("month", "cols")
    moves = [lambda c: c - 1, lambda c: c + 1, lambda c: c + ncols // 2, lambda c: c]
    shifts = [ncols - 1, 1, ncols // 2, 0]

    count = tile_count[0, 0]
    owner = (tile_rows[0] // own - my_cols) % ncols
    place = sum(jnp.where(owner == shift, d * own, 0) for d, shift in enumerate(shifts))
    slot = jnp.arange(tile_rows.shape[1], dtype=jnp.int32)
    row = jnp.where(slot < count, place + tile_rows[0] % own, 4 * own)
    slots = jnp.stack([row, tile_cols[0] % own])

    wet = jnp.broadcast_to(wet_mask(depth, block)[:, None, :], (own, SUB, block))
    wet = wet.reshape(own * SUB, block)
    force = padded(forcing[0], SUB)
    plates = pltpu.with_memory_space_constraint(tiles[0], pltpu.VMEM)

    arrived = None
    states = []
    for step in range(2 * months):
        month = months - 1 - step % months
        live = jnp.where(my_month == month, count, 0).reshape(1)
        terms, state = month_terms(live, slots, wet, force, plates, arrived)
        states.append(state)
        if step < 2 * months - 1:
            arrived = [
                lax.ppermute(term, axes, hops(month, months, ncols, move))
                for term, move in zip(terms, moves)
            ]

    held = states[-1]
    for month in range(1, months - 1):
        held = jnp.where(my_month == month, states[2 * months - 1 - month], held)
    passed = lax.ppermute(held, "month", [(m, (m + 1) % months) for m in range(months)])
    state = terms[3].astype(jnp.float32)
    for term, move in zip(terms[:3], moves):
        pairs = [(c, move(c) % ncols) for c in range(ncols)]
        state += lax.ppermute(term, "cols", pairs).astype(jnp.float32)
    result = jnp.where(my_month == 0, wet * state, passed)
    return result.reshape(1, own, SUB, block)[:, :, :tracers]


def solution(mesh):
    in_specs = (
        P("month", "cols", None, None),
        P("month", "cols", None, None),
        P("month", "cols"),
        P("month", "cols"),
        P("month", "cols"),
        P("cols", None),
    )
    out_specs = P("month", "cols", None, None)
    return jax.shard_map(
        on_device, mesh=mesh, in_specs=in_specs, out_specs=out_specs, check_vma=False
    )
```

```python
import functools

import jax
import jax.numpy as jnp
from jax import lax
from jax.experimental import pallas as pl
from jax.experimental.pallas import tpu as pltpu
from jax.sharding import PartitionSpec as P

SUB = 8
GROUP = 64
CHUNKS = 4
NT = (((1,), (1,)), ((), ()))
VMEM = pl.BlockSpec(memory_space=pltpu.VMEM)
SMEM = pl.BlockSpec(memory_space=pltpu.SMEM)
HBM = pl.BlockSpec(memory_space=pltpu.HBM)
LIVE, MONTH, NEAR, FAR = range(4)


def products(start, stop, table, tiles, x, acc):
    block = tiles.shape[-1]

    def round_of(g, carry):
        first = start + g * GROUP
        terms = []
        for u in range(0, GROUP, 2):
            s = first + u
            pair = jnp.concatenate([x[table[1, s]], x[table[1, s + 1]]], axis=0)
            both = tiles[pl.ds(s, 2)].reshape(2 * block, block)
            terms.append(
                lax.dot_general(pair.astype(jnp.bfloat16), both, NT, preferred_element_type=jnp.float32)
            )
        for u in range(0, GROUP, 2):
            s = first + u
            term = terms[u // 2]
            acc[table[0, s]] += term[:SUB, :block]
            acc[table[0, s + 1]] += term[SUB:, block:]
        return carry

    lax.fori_loop(0, (stop - start + GROUP - 1) // GROUP, round_of, 0)


def places(table, acc, own):
    nblk = acc.shape[0] - 1
    return table[2, FAR], table[2, NEAR], nblk // 2, 0


def clear(table, acc, own):
    for at in places(table, acc, own):
        acc[pl.ds(at, own)] = jnp.zeros((own,) + acc.shape[1:], acc.dtype)


def write_terms(table, acc, outs, own):
    for at, out in zip(places(table, acc, own), outs):
        out[...] = acc[pl.ds(at, own)].reshape(out.shape).astype(out.dtype)


def first_kernel(
    month, ncols, rows, cols, count, depth, forcing, tiles,
    o0, o1, o2, o3, kept, table, wet, force, x, acc, sems,
):
    own, width = depth.shape
    tracers, _, block = forcing.shape[1:]
    slots = tiles.shape[1]
    nblk = own * ncols
    size = slots // CHUNKS

    def load(i):
        part = pl.ds(i * size, size)
        return pltpu.make_async_copy(tiles.at[0, part], kept.at[part], sems.at[i])

    for i in range(CHUNKS):
        load(i).start()

    me = lax.axis_index("cols")
    my_month = lax.axis_index("month")
    live = count[0, 0]
    odd = lax.rem(me, 2) == 1
    table[2, LIVE] = live
    table[2, MONTH] = my_month
    table[2, NEAR] = jnp.where(odd, nblk - own, own)
    table[2, FAR] = jnp.where(odd, own, nblk - own)
    base = nblk - me * own

    def entry(s, carry):
        table[0, s] = jnp.where(s < live, lax.rem(rows[0, s] + base, nblk), nblk)
        table[1, s] = lax.rem(cols[0, s], own)
        return carry

    lax.fori_loop(0, slots, entry, 0, unroll=16)

    lane = lax.broadcasted_iota(jnp.int32, (width, block), 1)
    column = lax.broadcasted_iota(jnp.int32, (width, block), 0)
    spread = (lax.rem(lane, width) == column).astype(jnp.float32)
    below = jnp.dot(depth[...].astype(jnp.float32), spread, preferred_element_type=jnp.float32)
    level = lax.div(lax.broadcasted_iota(jnp.int32, (own, block), 1), width).astype(jnp.float32)
    wet[...] = jnp.broadcast_to((level < below).astype(jnp.float32)[:, None, :], wet.shape)
    force[...] = jnp.zeros_like(force)
    for t in range(tracers):
        force[:, t, :] = forcing[0, t]
    x[...] = force[...]
    clear(table, acc, own)

    for i in range(CHUNKS):
        load(i).wait()

        @pl.when((my_month == month) & (live > i * size))
        def _():
            products(i * size, jnp.minimum(live, (i + 1) * size), table, kept, x, acc)

    @pl.when(my_month == month)
    def _():
        write_terms(table, acc, (o0, o1, o2, o3), own)


def arrived_state(wet, arrived):
    total = arrived[0][...].astype(jnp.float32)
    for ref in arrived[1:]:
        total += ref[...].astype(jnp.float32)
    return total.reshape(wet.shape) * wet[...]


def step_kernel(month, table, wet, force, tiles, r0, r1, r2, r3, o0, o1, o2, o3, *refs):
    x, acc = refs[-2:]
    own = x.shape[0]

    @pl.when(table[2, MONTH] == month)
    def _():
        state = arrived_state(wet, (r0, r1, r2, r3))
        if len(refs) > 2:
            refs[0][...] = state
        x[...] = state + force[...]
        clear(table, acc, own)
        products(0, table[2, LIVE], table, tiles, x, acc)
        write_terms(table, acc, (o0, o1, o2, o3), own)


def last_kernel(table, wet, r0, r1, r2, r3, *refs):
    states, out = refs[:-1], refs[-1]
    month = table[2, MONTH]

    def put(state):
        for t in range(out.shape[1]):
            out[0, t] = state[:, t, :]

    for m, state in enumerate(states):

        @pl.when(month == m)
        def _():
            put(state[...])

    @pl.when(month == len(states))
    def _():
        put(arrived_state(wet, (r0, r1, r2, r3)))


def in_hbm(value):
    return pltpu.with_memory_space_constraint(value, pltpu.HBM)


def call(kernel, operands, in_specs, outs, out_specs, scratch):
    return pl.pallas_call(
        kernel,
        out_shape=outs,
        in_specs=in_specs,
        out_specs=out_specs,
        scratch_shapes=scratch,
        compiler_params=pltpu.CompilerParams(vmem_limit_bytes=12 * 2**20),
    )(*operands)


def idle_chain(active, months):
    to = (active - 1) % months
    if months != 4:
        return [(to - k) % months for k in range(1, months - 1)]
    if active ^ 1 == to:
        return [to ^ 2, to ^ 3]
    return [to ^ 1, active ^ 1]


def hops(active, months, ncols, move, whole):
    chain = [(active - 1) % months] + idle_chain(active, months) + [active]
    pairs = [(active * ncols + c, chain[0] * ncols + move(c)) for c in range(ncols)]
    if whole:
        for source, target in zip(chain, chain[1:]):
            pairs += [(source * ncols + c, target * ncols + c) for c in range(ncols)]
    return pairs


WHOLE = [True, True, True, True]
ORDER = [0, 1, 2, 3]


def on_device(forcing, tiles, tile_rows, tile_cols, tile_count, depth):
    months = lax.axis_size("month")
    ncols = lax.axis_size("cols")
    own, tracers, block = forcing.shape[1:]
    slots = tiles.shape[1]
    nblk = own * ncols
    far = lambda c: (c + 1) % ncols if c % 2 else (c - 1) % ncols
    near = lambda c: c ^ 1
    opposite = lambda c: (c + ncols // 2) % ncols
    moves = [far, near, opposite, lambda c: c]

    term = jax.ShapeDtypeStruct((own * SUB, block), jnp.bfloat16)
    plane = jax.ShapeDtypeStruct((own, SUB, block), jnp.float32)
    scratch = [
        pltpu.VMEM((own, SUB, block), jnp.float32),
        pltpu.VMEM((nblk + 1, SUB, block), jnp.float32),
    ]
    *terms, kept, table, wet, force = call(
        functools.partial(first_kernel, months - 1, ncols),
        (
            in_hbm(tile_rows),
            in_hbm(tile_cols),
            tile_count,
            in_hbm(depth),
            in_hbm(forcing.transpose(0, 2, 1, 3)),
            in_hbm(tiles),
        ),
        [SMEM, SMEM, SMEM, VMEM, VMEM, HBM],
        [term] * 4
        + [
            pltpu.VMEM(tiles.shape[1:], tiles.dtype),
            jax.ShapeDtypeStruct((3, slots), jnp.int32),
            plane,
            plane,
        ],
        [VMEM] * 5 + [SMEM, VMEM, VMEM],
        scratch + [pltpu.SemaphoreType.DMA((CHUNKS,))],
    )
    states = []
    for step in range(2 * months):
        month = months - 1 - step % months
        if step > 0:
            keep = step > months
            *terms, = call(
                functools.partial(step_kernel, month),
                (table, wet, force, kept, *arrived),
                [SMEM] + [VMEM] * 7,
                [term] * 4 + [plane] * keep,
                [VMEM] * (4 + keep),
                scratch,
            )
            if keep:
                states.insert(0, terms.pop())
        arrived = [None] * 4
        for k in ORDER:
            arrived[k] = lax.ppermute(
                terms[k], ("month", "cols"), hops(month, months, ncols, moves[k], WHOLE[k])
            )

    (held,) = call(
        last_kernel,
        (table, wet, *arrived, *states),
        [SMEM] + [VMEM] * (4 + months),
        [jax.ShapeDtypeStruct((1, tracers, own, block), jnp.float32)],
        [VMEM],
        [],
    )
    result = lax.ppermute(held, "month", [(m, (m + 1) % months) for m in range(months)])
    return result.transpose(0, 2, 1, 3)


def solution(mesh):
    in_specs = (
        P("month", "cols", None, None),
        P("month", "cols", None, None),
        P("month", "cols"),
        P("month", "cols"),
        P("month", "cols"),
        P("cols", None),
    )
    out_specs = P("month", "cols", None, None)
    return jax.shard_map(
        on_device, mesh=mesh, in_specs=in_specs, out_specs=out_specs, check_vma=False
    )
```

```python
import functools

import jax
import jax.numpy as jnp
from jax import lax
from jax.experimental import pallas as pl
from jax.experimental.pallas import tpu as pltpu
from jax.sharding import PartitionSpec as P

SUB = 8
GROUP = 64
NT = (((1,), (1,)), ((), ()))
VMEM = pl.BlockSpec(memory_space=pltpu.VMEM)
SMEM = pl.BlockSpec(memory_space=pltpu.SMEM)
HBM = pl.BlockSpec(memory_space=pltpu.HBM)
DMA = pltpu.SemaphoreType.DMA


def modulo(value, divisor):
    if divisor & (divisor - 1) == 0:
        return value & (divisor - 1)
    return lax.rem(value, divisor)


def rows_of(ref, index):
    return ref.at[pl.ds(pl.multiple_of(index * SUB, SUB), SUB)]


def products(start, stop, group, table, tiles, x, acc):
    block = tiles.shape[-1]

    def round_of(g, carry):
        first = start + g * group
        terms = []
        for u in range(0, group, 2):
            s = first + u
            pair = jnp.concatenate([rows_of(x, table[1, s])[...], rows_of(x, table[1, s + 1])[...]], axis=0)
            both = tiles[pl.ds(s, 2)].reshape(2 * block, block)
            terms.append(
                lax.dot_general(pair.astype(jnp.bfloat16), both, NT, preferred_element_type=jnp.float32)
            )
        for u in range(0, group, 2):
            s = first + u
            term = terms[u // 2]
            rows_of(acc, table[0, s])[...] += term[:SUB, :block]
            rows_of(acc, table[0, s + 1])[...] += term[SUB:, block:]
        return carry

    lax.fori_loop(0, (stop - start + group - 1) // group, round_of, 0)


def places(acc, own):
    nblk = acc.shape[0] // SUB - 1
    odd = lax.rem(lax.axis_index("cols"), 2) == 1
    return jnp.where(odd, own, nblk - own), nblk // 2, jnp.where(odd, nblk - own, own), 0


def clear(acc, own):
    for at in places(acc, own):
        acc[pl.ds(at * SUB, own * SUB)] = jnp.zeros((own * SUB, acc.shape[1]), acc.dtype)


def write_terms(acc, outs, own):
    for at, out in zip(places(acc, own), outs):
        for t in range(out.shape[0] // own):
            rows = acc[pl.ds(at * SUB + t, own, stride=SUB)]
            out[pl.ds(t * own, own)] = rows.astype(out.dtype)


def arrived_state(wet, arrived):
    total = arrived[0][...].astype(jnp.float32)
    for ref in arrived[1:]:
        total += ref[...].astype(jnp.float32)
    return total.reshape(-1, *wet.shape) * wet[...]


def set_x(x, values):
    x[...] = jnp.zeros_like(x)
    own = values.shape[1]
    for t in range(values.shape[0]):
        x[pl.ds(t, own, stride=SUB)] = values[t]


def taking(step, parts, tiles, kept, sems):
    size = kept.shape[0] // parts

    def load(i):
        part = pl.ds(i * size, size)
        return pltpu.make_async_copy(tiles.at[0, part], kept.at[part], sems.at[i])

    return size, load


def stream(step, parts, live, size, load, table, kept, x, acc):
    for i in range(parts):
        if i >= step:
            load(i).wait()

        @pl.when(live > i * size)
        def _():
            stop = jnp.minimum(live, (i + 1) * size)
            products(i * size, stop, min(size, GROUP), table, kept, x, acc)


def first_kernel(
    months, ncols, count, rows, cols, depth, forcing, tiles,
    o0, o1, o2, o3, kept, table, wet, force,
    x, acc, entries, rows_in, cols_in, depth_in, sems, own_sems,
):
    own, width = depth.shape
    block = forcing.shape[-1]
    nblk = own * ncols
    parts = months
    size, load = taking(0, parts, tiles, kept, sems)
    active = lax.axis_index("month") == months - 1

    small = [
        pltpu.make_async_copy(source, target, own_sems.at[i])
        for i, (source, target) in enumerate(
            [(rows, rows_in), (cols, cols_in), (depth, depth_in), (forcing, force)]
        )
    ]
    for copy in small:
        copy.start()
    load(0).start()

    @pl.when(active)
    def _():
        for i in range(1, parts):
            load(i).start()

    live = count[0, 0]
    base = nblk - lax.axis_index("cols") * own
    small[0].wait()
    small[1].wait()
    slot = lax.broadcasted_iota(jnp.int32, rows.shape, 1)
    entries[0:1, :] = jnp.where(slot < live, modulo(rows_in[...] + base, nblk), nblk)
    entries[1:2, :] = modulo(cols_in[...], own)
    entries[2:3, :] = jnp.full(rows.shape, live, jnp.int32)
    listing = pltpu.make_async_copy(entries, table, own_sems.at[4])
    listing.start()

    small[2].wait()
    small[3].wait()
    lane = lax.broadcasted_iota(jnp.int32, (width, block), 1)
    column = lax.broadcasted_iota(jnp.int32, (width, block), 0)
    spread = (lax.rem(lane, width) == column).astype(jnp.float32)
    below = jnp.dot(depth_in[...].astype(jnp.float32), spread, preferred_element_type=jnp.float32)
    level = lax.div(lax.broadcasted_iota(jnp.int32, (own, block), 1), width).astype(jnp.float32)
    wet[...] = (level < below).astype(jnp.float32)

    @pl.when(active)
    def _():
        set_x(x, force[0])
        clear(acc, own)

    listing.wait()

    @pl.when(active)
    def _():
        stream(0, parts, live, size, load, table, kept, x, acc)
        write_terms(acc, (o0, o1, o2, o3), own)

    @pl.when(jnp.logical_not(active))
    def _():
        load(0).wait()


def taking_kernel(
    step, months, table, wet, force, r0, r1, r2, r3, kept_in, tiles,
    o0, o1, o2, o3, kept, x, acc, sems,
):
    own = wet.shape[0]
    parts = months
    month = months - 1 - step
    size, load = taking(step, parts, tiles, kept, sems)
    my_month = lax.axis_index("month")

    @pl.when(my_month <= month)
    def _():
        load(step).start()

    @pl.when(my_month < month)
    def _():
        load(step).wait()

    @pl.when(my_month == month)
    def _():
        for i in range(step + 1, parts):
            load(i).start()
        set_x(x, arrived_state(wet, (r0, r1, r2, r3)) + force[0])
        clear(acc, own)
        stream(step, parts, table[2, 0], size, load, table, kept, x, acc)
        write_terms(acc, (o0, o1, o2, o3), own)


def step_kernel(
    month, table, wet, force, r0, r1, r2, r3, tiles,
    o0, o1, o2, o3, state, x, acc,
):
    own = wet.shape[0]

    @pl.when(lax.axis_index("month") == month)
    def _():
        arrived = arrived_state(wet, (r0, r1, r2, r3))
        state[0] = arrived
        set_x(x, arrived + force[0])
        clear(acc, own)
        products(0, table[2, 0], GROUP, table, tiles, x, acc)
        write_terms(acc, (o0, o1, o2, o3), own)


def held_kernel(*refs):
    states, out = refs[:-1], refs[-1]
    for m, state in enumerate(states):

        @pl.when(lax.axis_index("month") == m)
        def _():
            out[...] = state[...]


def last_kernel(wet, r0, r1, r2, r3, out):
    out[0] = arrived_state(wet, (r0, r1, r2, r3))


def in_hbm(value):
    return pltpu.with_memory_space_constraint(value, pltpu.HBM)


def call(kernel, operands, in_specs, outs, out_specs, scratch=(), aliases={}):
    return pl.pallas_call(
        kernel,
        out_shape=outs,
        in_specs=in_specs,
        out_specs=out_specs,
        scratch_shapes=list(scratch),
        input_output_aliases=aliases,
        compiler_params=pltpu.CompilerParams(vmem_limit_bytes=12 * 2**20),
    )(*operands)


def hops(k, active, target, months, ncols, move):
    if months != 4:
        ring = [target] + [m for m in range(months) if m not in (active, target)] + [active]
        then = dict(zip(ring, ring[1:]))
    elif active ^ 1 == target:
        mine, yours = active ^ 2, target ^ 2
        if k < 2:
            then = {target: yours, yours: mine, mine: active}
        else:
            then = {target: active, yours: mine, mine: yours}
    else:
        mine, yours = active ^ 1, target ^ 1
        then = {target: yours, yours: mine, mine: active}
    pairs = [(active * ncols + c, target * ncols + move(c)) for c in range(ncols)]
    for source, to in then.items():
        pairs += [(source * ncols + c, to * ncols + c) for c in range(ncols)]
    return pairs


def on_device(forcing, tiles, tile_rows, tile_cols, tile_count, depth):
    months = lax.axis_size("month")
    ncols = lax.axis_size("cols")
    own, tracers, block = forcing.shape[1:]
    slots = tiles.shape[1]
    nblk = own * ncols
    far = lambda c: (c + 1) % ncols if c % 2 else (c - 1) % ncols
    near = lambda c: c ^ 1
    opposite = lambda c: (c + ncols // 2) % ncols
    moves = [far, opposite, near, lambda c: c]

    term = jax.ShapeDtypeStruct((tracers * own, block), jnp.bfloat16)
    plane = jax.ShapeDtypeStruct((1, tracers, own, block), jnp.float32)
    mask = jax.ShapeDtypeStruct((own, block), jnp.float32)
    kept_like = pltpu.VMEM((slots, block, block), tiles.dtype)
    scratch = [
        pltpu.VMEM((own * SUB, block), jnp.float32),
        pltpu.VMEM(((nblk + 1) * SUB, block), jnp.float32),
    ]
    tiles = in_hbm(tiles)
    forcing = forcing.transpose(0, 2, 1, 3)
    *terms, kept, table, wet, force = call(
        functools.partial(first_kernel, months, ncols),
        (tile_count, in_hbm(tile_rows), in_hbm(tile_cols), in_hbm(depth), in_hbm(forcing), tiles),
        [SMEM] + [HBM] * 5,
        [term] * 4 + [kept_like, pltpu.SMEM((3, slots), jnp.int32), mask, plane],
        [VMEM] * 5 + [SMEM, VMEM, VMEM],
        scratch
        + [
            pltpu.VMEM((3, slots), jnp.int32),
            pltpu.VMEM(tile_rows.shape, jnp.int32),
            pltpu.VMEM(tile_cols.shape, jnp.int32),
            pltpu.VMEM(depth.shape, jnp.int32),
            DMA((months,)),
            DMA((5,)),
        ],
    )
    states = []
    for step in range(2 * months):
        month = months - 1 - step % months
        if 0 < step < months:
            *terms, kept = call(
                functools.partial(taking_kernel, step, months),
                (table, wet, force, *arrived, kept, tiles),
                [SMEM] + [VMEM] * 7 + [HBM],
                [term] * 4 + [kept_like],
                [VMEM] * 5,
                scratch + [DMA((months,))],
                {7: 4},
            )
        elif step > 0:
            *terms, state = call(
                functools.partial(step_kernel, month),
                (table, wet, force, *arrived, kept),
                [SMEM] + [VMEM] * 7,
                [term] * 4 + [plane],
                [VMEM] * 5,
                scratch,
            )
            states.insert(0, state)
        target = month - 1 if month else months - 1 if step < months else 1
        arrived = [
            lax.ppermute(term, ("month", "cols"), hops(k, month, target, months, ncols, move))
            for k, (term, move) in enumerate(zip(terms, moves))
        ]

    (held,) = call(held_kernel, states, [VMEM] * months, [plane], [VMEM])
    passed = lax.ppermute(held, "month", [(m, (m + 1) % months) for m in range(months)])
    (last,) = call(last_kernel, (wet, *arrived), [VMEM] * 5, [plane], [VMEM])
    crossed = lax.ppermute(last, "month", [(m, m ^ 1) for m in range(months)])
    result = jnp.where(lax.axis_index("month") == 0, crossed, passed)
    return result.transpose(0, 2, 1, 3)


def solution(mesh):
    in_specs = (
        P("month", "cols", None, None),
        P("month", "cols", None, None),
        P("month", "cols"),
        P("month", "cols"),
        P("month", "cols"),
        P("cols", None),
    )
    out_specs = P("month", "cols", None, None)
    return jax.shard_map(
        on_device, mesh=mesh, in_specs=in_specs, out_specs=out_specs, check_vma=False
    )
```

```python
import functools

import jax
import jax.numpy as jnp
from jax import lax
from jax.experimental import pallas as pl
from jax.experimental.pallas import tpu as pltpu
from jax.sharding import PartitionSpec as P

SUB = 8
PARTS = 4
GROUP = 64
NT = (((1,), (1,)), ((), ()))
VMEM = pl.BlockSpec(memory_space=pltpu.VMEM)
SMEM = pl.BlockSpec(memory_space=pltpu.SMEM)
HBM = pl.BlockSpec(memory_space=pltpu.HBM)
DMA = pltpu.SemaphoreType.DMA


def modulo(value, divisor):
    if divisor & (divisor - 1) == 0:
        return value & (divisor - 1)
    return lax.rem(value, divisor)


def rows_of(ref, index):
    return ref.at[pl.ds(pl.multiple_of(index * SUB, SUB), SUB)]


def products(start, stop, group, table, tiles, x, acc):
    block = tiles.shape[-1]

    def round_of(g, carry):
        first = start + g * group
        terms = []
        for u in range(0, group, 2):
            s = first + u
            pair = jnp.concatenate([rows_of(x, table[1, s])[...], rows_of(x, table[1, s + 1])[...]], axis=0)
            both = tiles[pl.ds(s, 2)].reshape(2 * block, block)
            terms.append(
                lax.dot_general(pair.astype(jnp.bfloat16), both, NT, preferred_element_type=jnp.float32)
            )
        for u in range(0, group, 2):
            s = first + u
            term = terms[u // 2]
            rows_of(acc, table[0, s])[...] += term[:SUB, :block]
            rows_of(acc, table[0, s + 1])[...] += term[SUB:, block:]
        return carry

    lax.fori_loop(0, (stop - start + group - 1) // group, round_of, 0)


def places(acc, own):
    nblk = acc.shape[0] // SUB - 1
    odd = lax.rem(lax.axis_index("cols"), 2) == 1
    return jnp.where(odd, own, nblk - own), nblk // 2, jnp.where(odd, nblk - own, own), 0


def clear(acc, own):
    for at in places(acc, own):
        acc[pl.ds(at * SUB, own * SUB)] = jnp.zeros((own * SUB, acc.shape[1]), acc.dtype)


def write_terms(acc, outs, own):
    for at, out in zip(places(acc, own), outs):
        for t in range(out.shape[0] // own):
            rows = acc[pl.ds(at * SUB + t, own, stride=SUB)]
            out[pl.ds(t * own, own)] = rows.astype(out.dtype)


def arrived_state(wet, arrived):
    total = arrived[0][...].astype(jnp.float32)
    for ref in arrived[1:]:
        total += ref[...].astype(jnp.float32)
    return total.reshape(-1, *wet.shape) * wet[...]


def set_x(x, values):
    x[...] = jnp.zeros_like(x)
    own = values.shape[1]
    for t in range(values.shape[0]):
        x[pl.ds(t, own, stride=SUB)] = values[t]


def stream(live, size, load, table, kept, x, acc):
    for i in range(PARTS):
        load(i).wait()

        @pl.when(live > i * size)
        def _():
            stop = jnp.minimum(live, (i + 1) * size)
            products(i * size, stop, min(size, GROUP), table, kept, x, acc)


def first_kernel(
    months, ncols, count, rows, cols, depth, forcing, tiles,
    o0, o1, o2, o3, kept, table, wet, force,
    x, acc, entries, rows_in, cols_in, depth_in, sems, own_sems,
):
    own, width = depth.shape
    block = forcing.shape[-1]
    nblk = own * ncols
    size = kept.shape[0] // PARTS

    def load(i):
        part = pl.ds(i * size, size)
        return pltpu.make_async_copy(tiles.at[0, part], kept.at[part], sems.at[i])

    active = lax.axis_index("month") == months - 1

    small = [
        pltpu.make_async_copy(source, target, own_sems.at[i])
        for i, (source, target) in enumerate(
            [(rows, rows_in), (cols, cols_in), (depth, depth_in), (forcing, force)]
        )
    ]
    for copy in small:
        copy.start()
    for i in range(PARTS):
        load(i).start()

    live = count[0, 0]
    base = nblk - lax.axis_index("cols") * own
    small[0].wait()
    small[1].wait()
    slot = lax.broadcasted_iota(jnp.int32, rows.shape, 1)
    entries[0:1, :] = jnp.where(slot < live, modulo(rows_in[...] + base, nblk), nblk)
    entries[1:2, :] = modulo(cols_in[...], own)
    entries[2:3, :] = jnp.full(rows.shape, live, jnp.int32)
    listing = pltpu.make_async_copy(entries, table, own_sems.at[4])
    listing.start()

    small[2].wait()
    small[3].wait()
    lane = lax.broadcasted_iota(jnp.int32, (width, block), 1)
    column = lax.broadcasted_iota(jnp.int32, (width, block), 0)
    spread = (lax.rem(lane, width) == column).astype(jnp.float32)
    below = jnp.dot(depth_in[...].astype(jnp.float32), spread, preferred_element_type=jnp.float32)
    level = lax.div(lax.broadcasted_iota(jnp.int32, (own, block), 1), width).astype(jnp.float32)
    wet[...] = (level < below).astype(jnp.float32)

    @pl.when(active)
    def _():
        set_x(x, force[0])
        clear(acc, own)

    listing.wait()

    @pl.when(active)
    def _():
        stream(live, size, load, table, kept, x, acc)
        write_terms(acc, (o0, o1, o2, o3), own)

    @pl.when(jnp.logical_not(active))
    def _():
        for i in range(PARTS):
            load(i).wait()


def step_kernel(
    month, table, wet, force, r0, r1, r2, r3, tiles,
    o0, o1, o2, o3, *refs,
):
    own = wet.shape[0]
    x, acc = refs[-2:]

    @pl.when(lax.axis_index("month") == month)
    def _():
        arrived = arrived_state(wet, (r0, r1, r2, r3))
        if len(refs) > 2:
            refs[0][0] = arrived
        set_x(x, arrived + force[0])
        clear(acc, own)
        products(0, table[2, 0], GROUP, table, tiles, x, acc)
        write_terms(acc, (o0, o1, o2, o3), own)


def held_kernel(*refs):
    states, out = refs[:-1], refs[-1]
    for m, state in enumerate(states):

        @pl.when(lax.axis_index("month") == m)
        def _():
            out[...] = state[...]


def last_kernel(wet, r0, r1, r2, r3, out):
    out[0] = arrived_state(wet, (r0, r1, r2, r3))


def in_hbm(value):
    return pltpu.with_memory_space_constraint(value, pltpu.HBM)


def call(kernel, operands, in_specs, outs, out_specs, scratch=()):
    return pl.pallas_call(
        kernel,
        out_shape=outs,
        in_specs=in_specs,
        out_specs=out_specs,
        scratch_shapes=list(scratch),
        compiler_params=pltpu.CompilerParams(vmem_limit_bytes=12 * 2**20),
    )(*operands)


def hops(k, active, target, months, ncols, move):
    if months != 4:
        ring = [target] + [m for m in range(months) if m not in (active, target)] + [active]
        then = dict(zip(ring, ring[1:]))
    elif active ^ 1 == target:
        mine, yours = active ^ 2, target ^ 2
        if k < 2:
            then = {target: yours, yours: mine, mine: active}
        else:
            then = {target: active, yours: mine, mine: yours}
    else:
        mine, yours = active ^ 1, target ^ 1
        then = {target: yours, yours: mine, mine: active}
        if k == 2:
            then = {target: active, yours: mine, mine: yours}
    pairs = [(active * ncols + c, target * ncols + move(c)) for c in range(ncols)]
    for source, to in then.items():
        pairs += [(source * ncols + c, to * ncols + c) for c in range(ncols)]
    return pairs


def on_device(forcing, tiles, tile_rows, tile_cols, tile_count, depth):
    months = lax.axis_size("month")
    ncols = lax.axis_size("cols")
    own, tracers, block = forcing.shape[1:]
    slots = tiles.shape[1]
    nblk = own * ncols
    far = lambda c: (c + 1) % ncols if c % 2 else (c - 1) % ncols
    near = lambda c: c ^ 1
    opposite = lambda c: (c + ncols // 2) % ncols
    moves = [far, opposite, near, lambda c: c]

    term = jax.ShapeDtypeStruct((tracers * own, block), jnp.bfloat16)
    plane = jax.ShapeDtypeStruct((1, tracers, own, block), jnp.float32)
    mask = jax.ShapeDtypeStruct((own, block), jnp.float32)
    kept_like = pltpu.VMEM((slots, block, block), tiles.dtype)
    scratch = [
        pltpu.VMEM((own * SUB, block), jnp.float32),
        pltpu.VMEM(((nblk + 1) * SUB, block), jnp.float32),
    ]
    tiles = in_hbm(tiles)
    forcing = forcing.transpose(0, 2, 1, 3)
    *terms, kept, table, wet, force = call(
        functools.partial(first_kernel, months, ncols),
        (tile_count, in_hbm(tile_rows), in_hbm(tile_cols), in_hbm(depth), in_hbm(forcing), tiles),
        [SMEM] + [HBM] * 5,
        [term] * 4 + [kept_like, pltpu.SMEM((3, slots), jnp.int32), mask, plane],
        [VMEM] * 5 + [SMEM, VMEM, VMEM],
        scratch
        + [
            pltpu.VMEM((3, slots), jnp.int32),
            pltpu.VMEM(tile_rows.shape, jnp.int32),
            pltpu.VMEM(tile_cols.shape, jnp.int32),
            pltpu.VMEM(depth.shape, jnp.int32),
            DMA((PARTS,)),
            DMA((5,)),
        ],
    )
    states = []
    for step in range(2 * months):
        month = months - 1 - step % months
        if step > 0:
            keep = step >= months
            result = call(
                functools.partial(step_kernel, month),
                (table, wet, force, *arrived, kept),
                [SMEM] + [VMEM] * 7,
                [term] * 4 + [plane] * keep,
                [VMEM] * (4 + keep),
                scratch,
            )
            terms, states = result[:4], list(result[4:]) + states
        target = month - 1 if month else months - 1 if step < months else 1
        arrived = [
            lax.ppermute(term, ("month", "cols"), hops(k, month, target, months, ncols, move))
            for k, (term, move) in enumerate(zip(terms, moves))
        ]

    (held,) = call(held_kernel, states, [VMEM] * months, [plane], [VMEM])
    passed = lax.ppermute(held, "month", [(m, (m + 1) % months) for m in range(months)])
    (last,) = call(last_kernel, (wet, *arrived), [VMEM] * 5, [plane], [VMEM])
    crossed = lax.ppermute(last, "month", [(m, m ^ 1) for m in range(months)])
    result = jnp.where(lax.axis_index("month") == 0, crossed, passed)
    return result.transpose(0, 2, 1, 3)


def solution(mesh):
    in_specs = (
        P("month", "cols", None, None),
        P("month", "cols", None, None),
        P("month", "cols"),
        P("month", "cols"),
        P("month", "cols"),
        P("cols", None),
    )
    out_specs = P("month", "cols", None, None)
    return jax.shard_map(
        on_device, mesh=mesh, in_specs=in_specs, out_specs=out_specs, check_vma=False
    )
```

```python
import functools

import jax
import jax.numpy as jnp
from jax import lax
from jax.experimental import pallas as pl
from jax.experimental.pallas import tpu as pltpu
from jax.sharding import PartitionSpec as P

SUB = 8
PARTS = 4
GROUP = 128
NT = (((1,), (1,)), ((), ()))
VMEM = pl.BlockSpec(memory_space=pltpu.VMEM)
SMEM = pl.BlockSpec(memory_space=pltpu.SMEM)
HBM = pl.BlockSpec(memory_space=pltpu.HBM)
DMA = pltpu.SemaphoreType.DMA


def modulo(value, divisor):
    if divisor & (divisor - 1) == 0:
        return value & (divisor - 1)
    return lax.rem(value, divisor)


def rows_of(ref, index):
    return ref.at[pl.ds(pl.multiple_of(index * SUB, SUB), SUB)]


def products(start, stop, group, table, tiles, x, acc):
    block = tiles.shape[-1]

    def round_of(g, carry):
        first = start + g * group
        terms = []
        for u in range(0, group, 2):
            s = first + u
            pair = jnp.concatenate([rows_of(x, table[1, s])[...], rows_of(x, table[1, s + 1])[...]], axis=0)
            both = tiles[pl.ds(s, 2)].reshape(2 * block, block)
            terms.append(
                lax.dot_general(pair.astype(jnp.bfloat16), both, NT, preferred_element_type=jnp.float32)
            )
        for u in range(0, group, 2):
            s = first + u
            term = terms[u // 2]
            rows_of(acc, table[0, s])[...] += term[:SUB, :block]
            rows_of(acc, table[0, s + 1])[...] += term[SUB:, block:]
        return carry

    lax.fori_loop(0, (stop - start + group - 1) // group, round_of, 0)


def places(acc, own):
    nblk = acc.shape[0] // SUB - 1
    odd = lax.rem(lax.axis_index("cols"), 2) == 1
    return jnp.where(odd, own, nblk - own), nblk // 2, jnp.where(odd, nblk - own, own), 0


def clear(acc, own):
    for at in places(acc, own):
        acc[pl.ds(at * SUB, own * SUB)] = jnp.zeros((own * SUB, acc.shape[1]), acc.dtype)


def write_terms(acc, outs, own):
    for at, out in zip(places(acc, own), outs):
        for t in range(out.shape[0] // own):
            rows = acc[pl.ds(at * SUB + t, own, stride=SUB)]
            out[pl.ds(t * own, own)] = rows.astype(out.dtype)


def arrived_state(wet, arrived):
    total = arrived[0][...].astype(jnp.float32)
    for ref in arrived[1:]:
        total += ref[...].astype(jnp.float32)
    return total.reshape(-1, *wet.shape) * wet[...]


def set_x(x, values):
    x[...] = jnp.zeros_like(x)
    own = values.shape[1]
    for t in range(values.shape[0]):
        x[pl.ds(t, own, stride=SUB)] = values[t]


def stream(live, size, load, table, kept, x, acc):
    for i in range(PARTS):
        load(i).wait()

        @pl.when(live > i * size)
        def _():
            stop = jnp.minimum(live, (i + 1) * size)
            products(i * size, stop, min(size, GROUP), table, kept, x, acc)


def first_kernel(
    months, ncols, count, rows, cols, depth, forcing, tiles,
    o0, o1, o2, o3, kept, table, wet, force,
    x, acc, entries, rows_in, cols_in, depth_in, sems, own_sems,
):
    own, width = depth.shape
    block = forcing.shape[-1]
    nblk = own * ncols
    size = kept.shape[0] // PARTS

    def load(i):
        part = pl.ds(i * size, size)
        return pltpu.make_async_copy(tiles.at[0, part], kept.at[part], sems.at[i])

    active = lax.axis_index("month") == months - 1

    small = [
        pltpu.make_async_copy(source, target, own_sems.at[i])
        for i, (source, target) in enumerate(
            [(rows, rows_in), (cols, cols_in), (depth, depth_in), (forcing, force)]
        )
    ]
    for copy in small:
        copy.start()
    for i in range(PARTS):
        load(i).start()

    live = count[0, 0]
    base = nblk - lax.axis_index("cols") * own
    small[0].wait()
    small[1].wait()
    slot = lax.broadcasted_iota(jnp.int32, rows.shape, 1)
    entries[0:1, :] = jnp.where(slot < live, modulo(rows_in[...] + base, nblk), nblk)
    entries[1:2, :] = modulo(cols_in[...], own)
    entries[2:3, :] = jnp.full(rows.shape, live, jnp.int32)
    listing = pltpu.make_async_copy(entries, table, own_sems.at[4])
    listing.start()

    small[2].wait()
    small[3].wait()
    lane = lax.broadcasted_iota(jnp.int32, (width, block), 1)
    column = lax.broadcasted_iota(jnp.int32, (width, block), 0)
    spread = (lax.rem(lane, width) == column).astype(jnp.float32)
    below = jnp.dot(depth_in[...].astype(jnp.float32), spread, preferred_element_type=jnp.float32)
    level = lax.div(lax.broadcasted_iota(jnp.int32, (own, block), 1), width).astype(jnp.float32)
    wet[...] = (level < below).astype(jnp.float32)

    @pl.when(active)
    def _():
        set_x(x, force[0])
        clear(acc, own)

    listing.wait()

    @pl.when(active)
    def _():
        stream(live, size, load, table, kept, x, acc)
        write_terms(acc, (o0, o1, o2, o3), own)

    @pl.when(jnp.logical_not(active))
    def _():
        for i in range(PARTS):
            load(i).wait()


def step_kernel(
    month, table, wet, force, r0, r1, r2, r3, tiles,
    o0, o1, o2, o3, *refs,
):
    own = wet.shape[0]
    x, acc = refs[-2:]

    @pl.when(lax.axis_index("month") == month)
    def _():
        arrived = arrived_state(wet, (r0, r1, r2, r3))
        if len(refs) > 2:
            refs[0][0] = arrived
        set_x(x, arrived + force[0])
        clear(acc, own)
        products(0, table[2, 0], GROUP, table, tiles, x, acc)
        write_terms(acc, (o0, o1, o2, o3), own)


def held_kernel(*refs):
    states, out = refs[:-1], refs[-1]
    for m, state in enumerate(states):

        @pl.when(lax.axis_index("month") == m)
        def _():
            out[...] = state[...]


def last_kernel(wet, r0, r1, r2, r3, out):
    out[0] = arrived_state(wet, (r0, r1, r2, r3))


def in_hbm(value):
    return pltpu.with_memory_space_constraint(value, pltpu.HBM)


def call(kernel, operands, in_specs, outs, out_specs, scratch=()):
    return pl.pallas_call(
        kernel,
        out_shape=outs,
        in_specs=in_specs,
        out_specs=out_specs,
        scratch_shapes=list(scratch),
        compiler_params=pltpu.CompilerParams(vmem_limit_bytes=12 * 2**20),
    )(*operands)


def hops(k, active, target, months, ncols, move):
    if months != 4:
        ring = [target] + [m for m in range(months) if m not in (active, target)] + [active]
        then = dict(zip(ring, ring[1:]))
    elif active ^ 1 == target:
        mine, yours = active ^ 2, target ^ 2
        if k < 2:
            then = {target: yours, yours: mine, mine: active}
        else:
            then = {target: active, yours: mine, mine: yours}
    else:
        mine, yours = active ^ 1, target ^ 1
        then = {target: yours, yours: mine, mine: active}
        if k == 2:
            then = {target: active, yours: mine, mine: yours}
    pairs = [(active * ncols + c, target * ncols + move(c)) for c in range(ncols)]
    for source, to in then.items():
        pairs += [(source * ncols + c, to * ncols + c) for c in range(ncols)]
    return pairs


def on_device(forcing, tiles, tile_rows, tile_cols, tile_count, depth):
    months = lax.axis_size("month")
    ncols = lax.axis_size("cols")
    own, tracers, block = forcing.shape[1:]
    slots = tiles.shape[1]
    nblk = own * ncols
    far = lambda c: (c + 1) % ncols if c % 2 else (c - 1) % ncols
    near = lambda c: c ^ 1
    opposite = lambda c: (c + ncols // 2) % ncols
    moves = [far, opposite, near, lambda c: c]

    term = jax.ShapeDtypeStruct((tracers * own, block), jnp.bfloat16)
    plane = jax.ShapeDtypeStruct((1, tracers, own, block), jnp.float32)
    mask = jax.ShapeDtypeStruct((own, block), jnp.float32)
    kept_like = pltpu.VMEM((slots, block, block), tiles.dtype)
    scratch = [
        pltpu.VMEM((own * SUB, block), jnp.float32),
        pltpu.VMEM(((nblk + 1) * SUB, block), jnp.float32),
    ]
    tiles = in_hbm(tiles)
    forcing = forcing.transpose(0, 2, 1, 3)
    *terms, kept, table, wet, force = call(
        functools.partial(first_kernel, months, ncols),
        (tile_count, in_hbm(tile_rows), in_hbm(tile_cols), in_hbm(depth), in_hbm(forcing), tiles),
        [SMEM] + [HBM] * 5,
        [term] * 4 + [kept_like, pltpu.SMEM((3, slots), jnp.int32), mask, plane],
        [VMEM] * 5 + [SMEM, VMEM, VMEM],
        scratch
        + [
            pltpu.VMEM((3, slots), jnp.int32),
            pltpu.VMEM(tile_rows.shape, jnp.int32),
            pltpu.VMEM(tile_cols.shape, jnp.int32),
            pltpu.VMEM(depth.shape, jnp.int32),
            DMA((PARTS,)),
            DMA((5,)),
        ],
    )
    states = []
    for step in range(2 * months):
        month = months - 1 - step % months
        if step > 0:
            keep = step >= months
            result = call(
                functools.partial(step_kernel, month),
                (table, wet, force, *arrived, kept),
                [SMEM] + [VMEM] * 7,
                [term] * 4 + [plane] * keep,
                [VMEM] * (4 + keep),
                scratch,
            )
            terms, states = result[:4], list(result[4:]) + states
        target = month - 1 if month else months - 1 if step < months else 1
        arrived = [
            lax.ppermute(term, ("month", "cols"), hops(k, month, target, months, ncols, move))
            for k, (term, move) in enumerate(zip(terms, moves))
        ]

    (held,) = call(held_kernel, states, [VMEM] * months, [plane], [VMEM])
    passed = lax.ppermute(held, "month", [(m, (m + 1) % months) for m in range(months)])
    (last,) = call(last_kernel, (wet, *arrived), [VMEM] * 5, [plane], [VMEM])
    crossed = lax.ppermute(last, "month", [(m, m ^ 1) for m in range(months)])
    result = jnp.where(lax.axis_index("month") == 0, crossed, passed)
    return result.transpose(0, 2, 1, 3)


def solution(mesh):
    in_specs = (
        P("month", "cols", None, None),
        P("month", "cols", None, None),
        P("month", "cols"),
        P("month", "cols"),
        P("month", "cols"),
        P("cols", None),
    )
    out_specs = P("month", "cols", None, None)
    return jax.shard_map(
        on_device, mesh=mesh, in_specs=in_specs, out_specs=out_specs, check_vma=False
    )
```
